256 devices in a mesh: gz: 8 (over y, x_hi), gy: 8 (over z), gx: 4 (over x_lo, core).
Axes of the slice: x: 4 (x_hi: 2, x_lo: 2; x = x_hi * 2 + x_lo), y: 4, z: 8, core: 2. Of those that a mesh axis runs over, the one named last changes fastest.
Arguments:
- phase: float32 [64, 1024, 512], P('gz', 'gy', 'gx'), may hold values from -1 to 1
- solute: float32 [64, 1024, 512], P('gz', 'gy', 'gx'), may hold values from -1 to 0.5
- advance: int32 [1], replicated, may hold values from 1 to 8
Outputs:
- phase_out: float32 [64, 1024, 512], P('gz', 'gy', 'gx')
- solute_out: float32 [64, 1024, 512], P('gz', 'gy', 'gx')
The draws below stay inside these ranges and needn't reach their ends.
All inputs are finite; a program needn't handle non-finite values.
Results may differ from the reference program's by a relative error of at most 0.00002.
Values sent between devices are 32-bit elements; how exact they have to be, the bound alone decides.
No kernel may reach another device: no remote copies, remote signals or barrier semaphores. Data moves between devices by JAX's collectives and lax.ppermute only.
A program may use at most 64 MiB of HBM per device.

```python
import jax
import jax.numpy as jnp
from jax import lax

CZ = 8
NZ = 64
NY = 1024
NX = 512


def steps_of(own_key, extent, pieces, least, high):
    loudness, own = 1.0, jax.random.fold_in(own_key, 6)
    for position, blocks in pieces:
        steps = jnp.exp(jax.random.uniform(jax.random.fold_in(own, position), (blocks,), jnp.float32, least / len(pieces), high / len(pieces)))
        loudness = loudness * jnp.repeat(steps, extent[position] // blocks).reshape([-1 if axis == position else 1 for axis in range(len(extent))])
    return loudness


def setup_inputs(seed: int = 0) -> dict:
    key_of = jax.random.split(jax.random.key(seed), 4)
    return {
        "phase": jnp.clip(jax.random.uniform(key_of[0], (NZ, NY, NX), jnp.float32, -1.0, 1.0) * steps_of(key_of[0], (NZ, NY, NX), ((0, 8), (1, 8), (2, 4)), -0.4, 0.0), -1.0, 1.0),
        "solute": jnp.clip(-1.0 + 1.5 * jax.random.uniform(key_of[1], (NZ, NY, NX), jnp.float32) ** steps_of(key_of[1], (NZ, NY, NX), ((0, 8), (1, 8), (2, 4)), -0.2, 0.2), -1.0, 0.5),
        "advance": jax.random.randint(key_of[2], (1,), 1, CZ + 1).astype(jnp.int32),
    }


E_ANI = 0.05
FLOOR = 0.5
LAM = 1.6
DT = 0.1
DSOL = 0.5
KPART = 0.15
GTH = 2.0


def padded(field):
    return jnp.pad(field, 1, mode="edge")


def neighbours(ext):
    return [ext[2:, 1:-1, 1:-1], ext[:-2, 1:-1, 1:-1], ext[1:-1, 2:, 1:-1],
            ext[1:-1, :-2, 1:-1], ext[1:-1, 1:-1, 2:], ext[1:-1, 1:-1, :-2]]


def anisotropy(ext):
    grad_z = (ext[2:, 1:-1, 1:-1] - ext[:-2, 1:-1, 1:-1]) * 0.5
    grad_y = (ext[1:-1, 2:, 1:-1] - ext[1:-1, :-2, 1:-1]) * 0.5
    grad_x = (ext[1:-1, 1:-1, 2:] - ext[1:-1, 1:-1, :-2]) * 0.5
    sq_z, sq_y, sq_x = grad_z * grad_z, grad_y * grad_y, grad_x * grad_x
    square = sq_z + sq_y + sq_x
    floor = jnp.maximum(square, FLOOR)
    ratio = (sq_z * sq_z + sq_y * sq_y + sq_x * sq_x) / (floor * floor)
    factor = 1.0 - 3.0 * E_ANI + 4.0 * E_ANI * ratio
    return factor * factor


def divergence(field_ext, coef_ext):
    centre_f = field_ext[1:-1, 1:-1, 1:-1]
    centre_c = coef_ext[1:-1, 1:-1, 1:-1]
    total = jnp.zeros_like(centre_f)
    for near_f, near_c in zip(neighbours(field_ext), neighbours(coef_ext)):
        total = total + 0.5 * (centre_c + near_c) * (near_f - centre_f)
    return total


def reference(phase, solute, advance):
    depth = phase.shape[0]
    phase_ext = padded(phase)
    aniso = anisotropy(phase_ext)
    lap = divergence(phase_ext, padded(aniso))
    planes = jnp.arange(depth, dtype=jnp.float32)
    thermal = (GTH * (planes + 0.5 - depth / 2.0) / depth)[:, None, None]
    force = lap + phase - phase * phase * phase - LAM * (1.0 - phase * phase) ** 2 * (solute + thermal)
    phase_new = jnp.clip(phase + DT * force / aniso, -1.0, 1.0)
    rate = (phase_new - phase) / DT
    mobility = DSOL * 0.5 * (1.0 - padded(phase_new))
    den = 0.5 * (1.0 + KPART) - 0.5 * (1.0 - KPART) * phase_new
    current = solute
    for sub in range(2):
        change = divergence(padded(current), mobility) + 0.5 * (1.0 + (1.0 - KPART) * current) * rate
        current = current + 0.5 * DT * change / den
    shift = advance[0].astype(jnp.int32)
    phase_full = jnp.concatenate([phase_new, -jnp.ones_like(phase_new)], axis=0)
    solute_full = jnp.concatenate([current, jnp.zeros_like(current)], axis=0)
    phase_out = lax.dynamic_slice_in_dim(phase_full, shift, depth, 0)
    solute_out = lax.dynamic_slice_in_dim(solute_full, shift, depth, 0)
    return phase_out, solute_out
```

```python
import functools

import jax
import jax.numpy as jnp
from jax import lax
from jax.experimental import pallas as pl
from jax.experimental.pallas import tpu as pltpu
from jax.sharding import PartitionSpec as P

E_ANI = 0.05
FLOOR = 0.5
LAM = 1.6
DT = 0.1
DSOL = 0.5
KPART = 0.15
GTH = 2.0

F32 = jnp.float32
DEPTH = 8
ROWS = 160
TILES = 18
VMEM = pl.BlockSpec(memory_space=pltpu.VMEM)
SMEM = pl.BlockSpec(memory_space=pltpu.SMEM)


def lanes():
    return lax.broadcasted_iota(jnp.int32, (8, 128), 1)


def sublanes():
    return lax.broadcasted_iota(jnp.int32, (8, 128), 0)


def swapped(v, step, axis, index):
    size = v.shape[axis]
    return jnp.where((index & step) != 0, pltpu.roll(v, step, axis), pltpu.roll(v, size - step, axis))


def reversed_bits(v, steps, axis, index):
    for step in steps:
        if 2 * step == v.shape[axis]:
            v = pltpu.roll(v, step, axis)
        else:
            v = swapped(v, step, axis, index)
    return v


def reciprocal(v):
    r = pl.reciprocal(v, approx=True)
    return r * (2.0 - v * r)


def pack_kernel(p_ref, u_ref, c_ref, up_ref, down_ref):
    group = lanes() >> 3
    sub = sublanes()
    for t in range(16):
        acc = jnp.zeros((8, 128), F32)
        for f, ref in enumerate((p_ref, u_ref)):
            for z in range(DEPTH):
                v = pltpu.roll(ref[z, 8 * t : 8 * t + 8, :], 64 * f + 8 * z + 4, 1)
                acc = jnp.where(group == 8 * f + z, v, acc)
        c_ref[8 * t : 8 * t + 8, :] = acc
    for z in range(DEPTH):
        up_ref[z] = jnp.where(sub >= 4, p_ref[z, 120:128, :], pltpu.roll(u_ref[z, 120:128, :], 4, 0))
        down_ref[z] = jnp.where(sub < 4, p_ref[z, 0:8, :], pltpu.roll(u_ref[z, 0:8, :], 4, 0))


def strips_kernel(info_ref, c_ref, left_ref, right_ref, up8_ref, down8_ref, s_ref, up_ref, down_ref):
    lane = lanes()
    low = (lane & 4) == 0
    first = info_ref[3] == 0
    last = info_ref[3] == info_ref[6] - 1
    mirror = (low & first) | (jnp.logical_not(low) & last)
    for t in range(16):
        rows = slice(8 * t, 8 * t + 8)
        v = jnp.where(low, left_ref[rows, :], right_ref[rows, :])
        own = reversed_bits(c_ref[rows, :], (1, 2, 4), 1, lane)
        v = jnp.where(mirror, own, v)
        s_ref[rows, :] = v
        if t == 0:
            down_ref[8] = v
        if t == 15:
            up_ref[8] = v
    up_ref[0:8] = up8_ref[...]
    down_ref[0:8] = down8_ref[...]


def halo_kernel(info_ref, from_up_ref, from_down_ref, up_ref, down_ref, s_ref, h_ref):
    sub = sublanes()
    low = sub < 4
    first = info_ref[2] == 0
    last = info_ref[2] == info_ref[5] - 1
    for z in range(9):
        below = jnp.where(first, reversed_bits(down_ref[z], (1, 2, 4), 0, sub), from_up_ref[z])
        above = jnp.where(last, reversed_bits(up_ref[z], (1, 2, 4), 0, sub), from_down_ref[z])
        v = jnp.where(low, above, below)
        if z < 8:
            h_ref[z] = v
            h_ref[8 + z] = pltpu.roll(jnp.where(low, below, above), 4, 0)
        else:
            h_ref[32] = v
    for t in range(16):
        h_ref[16 + t] = s_ref[8 * t : 8 * t + 8, :]


def step_kernel(
    early,
    info_ref,
    p_ref,
    u_ref,
    pn_ref,
    un_ref,
    ex_ref,
    h_ref,
    hn_ref,
    hx_ref,
    phase_ref,
    solute_ref,
    pb,
    ub,
    ab,
    nb,
    db,
    rb,
    sb,
    edges,
    strips,
):
    shift = info_ref[0]
    gz = info_ref[1]
    count_z = info_ref[4]
    total = DEPTH * count_z
    lane = lanes()
    group = lane >> 3
    low = (lane & 4) == 0
    at0 = lane == 0
    at127 = lane == 127
    is_first = gz == 0
    is_last = gz == count_z - 1
    is_second = gz == count_z - 2

    def place(buf, pos, src, index, h, base):
        buf[pos, 16:144, :] = src[index]
        edge = h[base]
        buf[pos, 8:16, :] = edge
        buf[pos, 144:152, :] = edge

    extra_p = 3 if early else 4
    extra_u = 1 if early else 2
    for z in range(DEPTH):
        place(pb, z, p_ref, z, h_ref, z)
        place(ub, z, u_ref, z, h_ref, 8 + z)
    for z in range(pn_ref.shape[0]):
        place(pb, 8 + z, pn_ref, z, hn_ref, z)
    for z in range(un_ref.shape[0]):
        place(ub, 8 + z, un_ref, z, hn_ref, 8 + z)
    for j in range(extra_p):
        pos = 13 + j if early else j
        taken = pos >= 12 + shift if early else pos <= shift - 5

        @pl.when(taken)
        def _():
            place(pb, pos, ex_ref, j, hx_ref, 5 + j if early else j)

    for j in range(extra_u):
        pos = 15 if early else j
        taken = pos >= 14 + shift if early else pos <= shift - 7

        @pl.when(taken)
        def _():
            place(ub, pos, ex_ref, extra_p + j, hx_ref, 8 + (7 if early else j))

    for pos in (12, 13, 14, 15) if early else (0, 1, 2, 3):
        taken = (pos >= 12 + shift) & is_first if early else (pos <= shift - 5) & is_second

        @pl.when(taken)
        def _():
            pb[pos, 8:152, :] = pb[15 - pos, 8:152, :]
            ub[pos, 8:152, :] = ub[15 - pos, 8:152, :]

    @pl.when(is_last)
    def _():
        for pos in (8, 9, 10, 11):
            pb[pos, 8:152, :] = pb[15 - pos, 8:152, :]
            ub[pos, 8:152, :] = ub[15 - pos, 8:152, :]

    fresh = group >= 12 + shift if early else group <= shift - 5
    mirror = (is_last & (group >= 8) & (group < 12)) | (fresh & (is_first if early else is_second))
    for t in range(TILES):
        src = 32 if t in (0, TILES - 1) else 15 + t
        own, near, far = h_ref[src], hn_ref[src], hx_ref[src]
        own_r, near_r, far_r = (pltpu.roll(v, 64, 1) for v in (own, near, far))
        cp = jnp.where(group < 8, own, near_r)
        cu = jnp.where(group < 8, own_r, near)
        cp = jnp.where(fresh, far_r if early else far, cp)
        cu = jnp.where(fresh, far if early else far_r, cu)
        cp = jnp.where(mirror, reversed_bits(cp, (8, 16, 32, 64), 1, lane), cp)
        cu = jnp.where(mirror, reversed_bits(cu, (8, 16, 32, 64), 1, lane), cu)
        rows = slice(8 + 8 * t, 16 + 8 * t)
        edges[0, rows, :] = cp
        edges[1, rows, :] = cu
        gp = jnp.zeros((8, 128), F32)
        gu = jnp.zeros((8, 128), F32)
        for pos in range(16):
            gp = jnp.where(group == pos, pltpu.roll(pb[pos, rows, :], 8 * pos + 4, 1), gp)
            gu = jnp.where(group == pos, pltpu.roll(ub[pos, rows, :], 8 * pos + 4, 1), gu)
        strips[0, 0, rows, :] = jnp.where(low, cp, gp)
        strips[0, 1, rows, :] = jnp.where(low, gp, cp)
        strips[1, 0, rows, :] = jnp.where(low, cu, gu)
        strips[1, 1, rows, :] = jnp.where(low, gu, cu)

    def aniso_of(dz, dy, dx):
        sz, sy, sx = dz * dz, dy * dy, dx * dx
        floor = jnp.maximum(sz + sy + sx, 4.0 * FLOOR)
        ratio = (sz * sz + sy * sy + sx * sx) * reciprocal(floor * floor)
        factor = (1.0 - 3.0 * E_ANI) + (4.0 * E_ANI) * ratio
        return factor * factor

    def flux_sum(f, c, fs, cs):
        acc = None
        for near_f, near_c in zip(fs, cs):
            term = (c + near_c) * (near_f - f)
            acc = term if acc is None else acc + term
        return acc

    def phase_of(p, a, u, total_flux, thermal):
        om = 1.0 - p * p
        force = 0.5 * total_flux + om * (p - LAM * om * (u + thermal))
        new = jnp.clip(p + DT * (force * reciprocal(a)), -1.0, 1.0)
        den = 0.5 * (1.0 + KPART) - 0.5 * (1.0 - KPART) * new
        return 1.0 - new, new - p, 0.125 * DT * DSOL * reciprocal(den)

    def solute_of(u, d, r, total_flux):
        k = 0.5 / DT / (0.25 * DSOL)
        return u + r * (total_flux + (k + k * (1.0 - KPART) * u) * d)

    def thermal_of(g):
        g = jnp.where(g < 0, -1 - g, g)
        g = jnp.where(g >= total, 2 * total - 1 - g, g)
        return (GTH * (g.astype(F32) + 0.5 - total.astype(F32) / 2.0)) / total.astype(F32)

    q_lane = shift - 4 + ((group - (shift - 4)) & 15)
    strip_thermal = thermal_of(DEPTH * gz + q_lane)

    def strip_near(field, side, r0):
        v = strips[field, side, r0 : r0 + 8, :]
        return v, (
            pltpu.roll(v, 120, 1),
            pltpu.roll(v, 8, 1),
            strips[field, side, r0 + 1 : r0 + 9, :],
            strips[field, side, r0 - 1 : r0 + 7, :],
            pltpu.roll(v, 127, 1),
            pltpu.roll(v, 1, 1),
        )

    def strip_stage(fn, edge):
        for t in range(TILES):
            r0 = 8 + 8 * t
            left = fn(0, r0)
            right = fn(1, r0)
            edges[edge, r0 : r0 + 8, :] = jnp.where(low, left, right)

    def strip_aniso(side, r0):
        _, n = strip_near(0, side, r0)
        a = aniso_of(n[0] - n[1], n[2] - n[3], n[4] - n[5])
        strips[2, side, r0 : r0 + 8, :] = a
        return a

    def strip_phase(side, r0):
        p, ps = strip_near(0, side, r0)
        a, as_ = strip_near(2, side, r0)
        u = strips[1, side, r0 : r0 + 8, :]
        n, d, r = phase_of(p, a, u, flux_sum(p, a, ps, as_), strip_thermal)
        strips[3, side, r0 : r0 + 8, :] = n
        strips[4, side, r0 : r0 + 8, :] = d
        strips[5, side, r0 : r0 + 8, :] = r
        return n

    def strip_solute(side, r0):
        u, us = strip_near(1, side, r0)
        n, ns = strip_near(3, side, r0)
        d = strips[4, side, r0 : r0 + 8, :]
        r = strips[5, side, r0 : r0 + 8, :]
        return solute_of(u, d, r, flux_sum(u, n, us, ns))

    strip_stage(strip_aniso, 2)
    strip_stage(strip_phase, 3)
    strip_stage(strip_solute, 4)

    def near(buf, edge, q, r0):
        p = q & 15
        v = buf[p, r0 : r0 + 8, :]
        e = pltpu.roll(edges[edge, r0 : r0 + 8, :], 124 - 8 * p, 1)
        return v, (
            buf[(q + 1) & 15, r0 : r0 + 8, :],
            buf[(q - 1) & 15, r0 : r0 + 8, :],
            buf[p, r0 + 1 : r0 + 9, :],
            buf[p, r0 - 1 : r0 + 7, :],
            pltpu.roll(jnp.where(at0, e, v), 127, 1),
            pltpu.roll(jnp.where(at127, e, v), 1, 1),
        )

    def stage(first, count, tiles, fn):
        def step(i, carry):
            for t in tiles:
                fn(shift + first + i, 8 + 8 * t)
            return carry

        lax.fori_loop(0, count, step, 0)

    def plane_aniso(q, r0):
        _, n = near(pb, 0, q, r0)
        ab[q & 15, r0 : r0 + 8, :] = aniso_of(n[0] - n[1], n[2] - n[3], n[4] - n[5])

    def plane_phase(q, r0):
        p, ps = near(pb, 0, q, r0)
        a, as_ = near(ab, 2, q, r0)
        u = ub[q & 15, r0 : r0 + 8, :]
        n, d, r = phase_of(p, a, u, flux_sum(p, a, ps, as_), thermal_of(DEPTH * gz + q))
        nb[q & 15, r0 : r0 + 8, :] = n
        db[q & 15, r0 : r0 + 8, :] = d
        rb[q & 15, r0 : r0 + 8, :] = r

    def substep(buf, edge, q, r0):
        u, us = near(buf, edge, q, r0)
        n, ns = near(nb, 3, q, r0)
        return n, solute_of(u, db[q & 15, r0 : r0 + 8, :], rb[q & 15, r0 : r0 + 8, :], flux_sum(u, n, us, ns))

    def plane_first(q, r0):
        _, v = substep(ub, 1, q, r0)
        sb[q & 15, r0 : r0 + 8, :] = v

    def plane_second(q, r0):
        n, v = substep(sb, 4, q, r0)
        outside = DEPTH * gz + q >= total
        phase_ref[q - shift, r0 - 16 : r0 - 8, :] = jnp.where(outside, -1.0, 1.0 - n)
        solute_ref[q - shift, r0 - 16 : r0 - 8, :] = jnp.where(outside, 0.0, v)

    every = range(TILES)
    stage(-3, 14, every, plane_aniso)
    stage(-2, 12, every, plane_phase)
    stage(-1, 10, every, plane_first)
    stage(0, 8, range(1, TILES - 1), plane_second)


def moved(value, axis, steps):
    count = lax.axis_size(axis)
    first, last = (max(0, -steps), min(count, count - steps))
    return lax.ppermute(value, axis, [(source, source + steps) for source in range(first, last)])


def out(*shape):
    return jax.ShapeDtypeStruct(shape, F32)


def call(kernel, shapes, n_smem, *args, scratch=()):
    return pl.pallas_call(
        kernel,
        out_shape=shapes,
        in_specs=[SMEM] * n_smem + [VMEM] * (len(args) - n_smem),
        out_specs=jax.tree.map(lambda _: VMEM, shapes),
        scratch_shapes=scratch,
        compiler_params=pltpu.CompilerParams(vmem_limit_bytes=40 * 1024 * 1024),
    )(*args)


def branch(early, phase, solute, info):
    near_p = moved(phase[0:7] if early else phase, "gz", -1)
    near_u = moved(solute[0:5] if early else solute, "gz", -1)
    if early:
        extra = moved(jnp.concatenate([phase[5:8], solute[7:8]]), "gz", 1)
    else:
        extra = moved(jnp.concatenate([phase[0:4], solute[0:2]]), "gz", -2)
    own_c, up8, down8 = call(pack_kernel, (out(128, 128), out(8, 8, 128), out(8, 8, 128)), 0, phase, solute)
    left = moved(own_c, "gx", 1)
    right = moved(own_c, "gx", -1)
    strip, up, down = call(
        strips_kernel, (out(128, 128), out(9, 8, 128), out(9, 8, 128)), 1, info, own_c, left, right, up8, down8
    )
    from_up = moved(up, "gy", 1)
    from_down = moved(down, "gy", -1)
    halo = call(halo_kernel, out(33, 8, 128), 1, info, from_up, from_down, up, down, strip)
    near_h = moved(halo, "gz", -1)
    extra_h = moved(halo, "gz", 1 if early else -2)
    whole = pltpu.VMEM((16, ROWS, 128), F32)
    return call(
        functools.partial(step_kernel, early),
        (out(*phase.shape), out(*phase.shape)),
        1,
        info,
        phase,
        solute,
        near_p,
        near_u,
        extra,
        halo,
        near_h,
        extra_h,
        scratch=[whole] * 7 + [pltpu.VMEM((5, ROWS, 128), F32), pltpu.VMEM((6, 2, ROWS, 128), F32)],
    )


def body(phase, solute, advance):
    axes = ("gz", "gy", "gx")
    info = jnp.stack(
        [advance[0]] + [lax.axis_index(a) for a in axes] + [jnp.int32(lax.axis_size(a)) for a in axes]
    ).astype(jnp.int32)
    return lax.cond(
        advance[0] < 4, functools.partial(branch, True), functools.partial(branch, False), phase, solute, info
    )


def solution(mesh):
    in_specs = (P("gz", "gy", "gx"), P("gz", "gy", "gx"), P())
    out_specs = (P("gz", "gy", "gx"), P("gz", "gy", "gx"))
    return jax.shard_map(body, mesh=mesh, in_specs=in_specs, out_specs=out_specs, check_vma=False)
```

```python
import functools

import jax
import jax.numpy as jnp
from jax import lax
from jax.experimental import pallas as pl
from jax.experimental.pallas import tpu as pltpu
from jax.sharding import PartitionSpec as P

E_ANI = 0.05
FLOOR = 0.5
LAM = 1.6
DT = 0.1
DSOL = 0.5
KPART = 0.15
GTH = 2.0

F32 = jnp.float32
DEPTH = 8
ROWS = 160
TILES = 18
VMEM = pl.BlockSpec(memory_space=pltpu.VMEM)
SMEM = pl.BlockSpec(memory_space=pltpu.SMEM)


def lanes():
    return lax.broadcasted_iota(jnp.int32, (8, 128), 1)


def sublanes():
    return lax.broadcasted_iota(jnp.int32, (8, 128), 0)


def swapped(v, step, axis, index):
    size = v.shape[axis]
    return jnp.where((index & step) != 0, pltpu.roll(v, step, axis), pltpu.roll(v, size - step, axis))


def reversed_bits(v, steps, axis, index):
    for step in steps:
        if 2 * step == v.shape[axis]:
            v = pltpu.roll(v, step, axis)
        else:
            v = swapped(v, step, axis, index)
    return v


def reciprocal(v):
    r = pl.reciprocal(v, approx=True)
    return r * (2.0 - v * r)


def pack_kernel(p_ref, u_ref, c_ref, up_ref, down_ref):
    group = lanes() >> 3
    sub = sublanes()
    for t in range(16):
        acc = jnp.zeros((8, 128), F32)
        for f, ref in enumerate((p_ref, u_ref)):
            for z in range(DEPTH):
                v = pltpu.roll(ref[z, 8 * t : 8 * t + 8, :], 64 * f + 8 * z + 4, 1)
                acc = jnp.where(group == 8 * f + z, v, acc)
        c_ref[8 * t : 8 * t + 8, :] = acc
    for z in range(DEPTH):
        up_ref[z] = jnp.where(sub >= 4, p_ref[z, 120:128, :], pltpu.roll(u_ref[z, 120:128, :], 4, 0))
        down_ref[z] = jnp.where(sub < 4, p_ref[z, 0:8, :], pltpu.roll(u_ref[z, 0:8, :], 4, 0))


def strips_kernel(info_ref, c_ref, left_ref, right_ref, up8_ref, down8_ref, s_ref, up_ref, down_ref):
    lane = lanes()
    low = (lane & 4) == 0
    first = info_ref[3] == 0
    last = info_ref[3] == info_ref[6] - 1
    mirror = (low & first) | (jnp.logical_not(low) & last)
    for t in range(16):
        rows = slice(8 * t, 8 * t + 8)
        v = jnp.where(low, left_ref[rows, :], right_ref[rows, :])
        own = reversed_bits(c_ref[rows, :], (1, 2, 4), 1, lane)
        v = jnp.where(mirror, own, v)
        s_ref[rows, :] = v
        if t == 0:
            down_ref[8] = v
        if t == 15:
            up_ref[8] = v
    up_ref[0:8] = up8_ref[...]
    down_ref[0:8] = down8_ref[...]


def halo_kernel(info_ref, from_up_ref, from_down_ref, up_ref, down_ref, s_ref, h_ref):
    sub = sublanes()
    low = sub < 4
    first = info_ref[2] == 0
    last = info_ref[2] == info_ref[5] - 1
    for z in range(9):
        below = jnp.where(first, reversed_bits(down_ref[z], (1, 2, 4), 0, sub), from_up_ref[z])
        above = jnp.where(last, reversed_bits(up_ref[z], (1, 2, 4), 0, sub), from_down_ref[z])
        v = jnp.where(low, above, below)
        if z < 8:
            h_ref[z] = v
            h_ref[8 + z] = pltpu.roll(jnp.where(low, below, above), 4, 0)
        else:
            h_ref[32] = v
    for t in range(16):
        h_ref[16 + t] = s_ref[8 * t : 8 * t + 8, :]


def step_kernel(
    early,
    info_ref,
    p_ref,
    u_ref,
    pn_ref,
    un_ref,
    ex_ref,
    h_ref,
    hn_ref,
    hx_ref,
    phase_ref,
    solute_ref,
    pb,
    ub,
    ab,
    nb,
    db,
    rb,
    sb,
    pl_b,
    pr_b,
    nl_b,
    nr_b,
    *more,
):
    edges, strips = more[:5], more[5:]
    shift = info_ref[0]
    gz = info_ref[1]
    count_z = info_ref[4]
    total = DEPTH * count_z
    lane = lanes()
    group = lane >> 3
    low = (lane & 4) == 0
    at0 = lane == 0
    at127 = lane == 127
    is_first = gz == 0
    is_last = gz == count_z - 1
    is_second = gz == count_z - 2

    def place(buf, pos, src, index, h, base):
        buf[pos, 16:144, :] = src[index]
        edge = h[base]
        buf[pos, 8:16, :] = edge
        buf[pos, 144:152, :] = edge

    extra_p = 3 if early else 4
    extra_u = 1 if early else 2
    for z in range(DEPTH):
        place(pb, z, p_ref, z, h_ref, z)
        place(ub, z, u_ref, z, h_ref, 8 + z)
    for z in range(pn_ref.shape[0]):
        place(pb, 8 + z, pn_ref, z, hn_ref, z)
    for z in range(un_ref.shape[0]):
        place(ub, 8 + z, un_ref, z, hn_ref, 8 + z)
    for j in range(extra_p):
        pos = 13 + j if early else j
        taken = pos >= 12 + shift if early else pos <= shift - 5

        @pl.when(taken)
        def _():
            place(pb, pos, ex_ref, j, hx_ref, 5 + j if early else j)

    for j in range(extra_u):
        pos = 15 if early else j
        taken = pos >= 14 + shift if early else pos <= shift - 7

        @pl.when(taken)
        def _():
            place(ub, pos, ex_ref, extra_p + j, hx_ref, 8 + (7 if early else j))

    for pos in (12, 13, 14, 15) if early else (0, 1, 2, 3):
        taken = (pos >= 12 + shift) & is_first if early else (pos <= shift - 5) & is_second

        @pl.when(taken)
        def _():
            pb[pos, 8:152, :] = pb[15 - pos, 8:152, :]
            ub[pos, 8:152, :] = ub[15 - pos, 8:152, :]

    @pl.when(is_last)
    def _():
        for pos in (8, 9, 10, 11):
            pb[pos, 8:152, :] = pb[15 - pos, 8:152, :]
            ub[pos, 8:152, :] = ub[15 - pos, 8:152, :]

    fresh = group >= 12 + shift if early else group <= shift - 5
    mirror = (is_last & (group >= 8) & (group < 12)) | (fresh & (is_first if early else is_second))
    for t in range(TILES):
        src = 32 if t in (0, TILES - 1) else 15 + t
        own, near, far = h_ref[src], hn_ref[src], hx_ref[src]
        own_r, near_r, far_r = (pltpu.roll(v, 64, 1) for v in (own, near, far))
        cp = jnp.where(group < 8, own, near_r)
        cu = jnp.where(group < 8, own_r, near)
        rows = slice(8 + 8 * t, 16 + 8 * t)
        edges[0][rows, :] = jnp.where(fresh, far_r if early else far, cp)
        edges[1][rows, :] = jnp.where(fresh, far if early else far_r, cu)

    @pl.when(is_last | (is_first if early else is_second))
    def _():
        back = is_first if early else False
        pick = (lane >> 3) & 3
        for t in range(TILES):
            rows = slice(8 + 8 * t, 16 + 8 * t)
            for field in (0, 1):
                v = edges[field][rows, :]
                m = v
                for j in range(4):
                    amount = 8 * (2 * j + 1)
                    if early:
                        turned = pltpu.roll(v, jnp.where(back, 128 - amount, amount), 1)
                        m = jnp.where(pick == jnp.where(back, 3 - j, j), turned, m)
                    else:
                        m = jnp.where(pick == j, pltpu.roll(v, amount, 1), m)
                edges[field][rows, :] = jnp.where(mirror, m, v)

    for t in range(TILES):
        rows = slice(8 + 8 * t, 16 + 8 * t)
        cp = edges[0][rows, :]
        cu = edges[1][rows, :]
        gp = jnp.zeros((8, 128), F32)
        gu = jnp.zeros((8, 128), F32)
        for pos in range(16):
            gp = jnp.where(group == pos, pltpu.roll(pb[pos, rows, :], 8 * pos + 4, 1), gp)
        for pos in range(16):
            gu = jnp.where(group == pos, pltpu.roll(ub[pos, rows, :], 8 * pos + 4, 1), gu)
        strips[0][rows, :] = jnp.where(low, cp, gp)
        strips[1][rows, :] = jnp.where(low, gp, cp)
        strips[2][rows, :] = jnp.where(low, cu, gu)
        strips[3][rows, :] = jnp.where(low, gu, cu)

    def aniso_of(dz, dy, dx):
        sz, sy, sx = dz * dz, dy * dy, dx * dx
        floor = jnp.maximum(sz + sy + sx, 4.0 * FLOOR)
        ratio = (sz * sz + sy * sy + sx * sx) * reciprocal(floor * floor)
        factor = (1.0 - 3.0 * E_ANI) + (4.0 * E_ANI) * ratio
        return factor * factor

    def flux_sum(f, c, fs, cs):
        acc = None
        for near_f, near_c in zip(fs, cs):
            term = (c + near_c) * (near_f - f)
            acc = term if acc is None else acc + term
        return acc

    def phase_of(p, a, u, total_flux, thermal):
        om = 1.0 - p * p
        force = 0.5 * total_flux + om * (p - LAM * om * (u + thermal))
        new = jnp.clip(p + DT * (force * reciprocal(a)), -1.0, 1.0)
        den = 0.5 * (1.0 + KPART) - 0.5 * (1.0 - KPART) * new
        return 1.0 - new, new - p, 0.125 * DT * DSOL * reciprocal(den)

    def solute_of(u, d, r, total_flux):
        k = 0.5 / DT / (0.25 * DSOL)
        return u + r * (total_flux + (k + k * (1.0 - KPART) * u) * d)

    def thermal_of(g):
        g = jnp.where(g < 0, -1 - g, g)
        g = jnp.where(g >= total, 2 * total - 1 - g, g)
        return (GTH * (g.astype(F32) + 0.5 - total.astype(F32) / 2.0)) / total.astype(F32)

    q_lane = shift - 4 + ((group - (shift - 4)) & 15)
    strip_thermal = thermal_of(DEPTH * gz + q_lane)

    def strip_near(field, side, r0):
        v = strips[2 * field + side][r0 : r0 + 8, :]
        return v, (
            pltpu.roll(v, 120, 1),
            pltpu.roll(v, 8, 1),
            strips[2 * field + side][r0 + 1 : r0 + 9, :],
            strips[2 * field + side][r0 - 1 : r0 + 7, :],
            pltpu.roll(v, 127, 1),
            pltpu.roll(v, 1, 1),
        )

    def strip_stage(fn, edge):
        for t in range(TILES):
            r0 = 8 + 8 * t
            edges[edge][r0 : r0 + 8, :] = jnp.where(low, fn(0, r0), fn(1, r0))

    def strip_aniso(side, r0):
        _, n = strip_near(0, side, r0)
        a = aniso_of(n[0] - n[1], n[2] - n[3], n[4] - n[5])
        strips[4 + side][r0 : r0 + 8, :] = a
        return a

    def strip_phase(side, r0):
        p, ps = strip_near(0, side, r0)
        a, as_ = strip_near(2, side, r0)
        u = strips[2 + side][r0 : r0 + 8, :]
        n, d, r = phase_of(p, a, u, flux_sum(p, a, ps, as_), strip_thermal)
        strips[6 + side][r0 : r0 + 8, :] = n
        strips[8 + side][r0 : r0 + 8, :] = d
        strips[10 + side][r0 : r0 + 8, :] = r
        return n

    def strip_solute(side, r0):
        u, us = strip_near(1, side, r0)
        n, ns = strip_near(3, side, r0)
        d = strips[8 + side][r0 : r0 + 8, :]
        r = strips[10 + side][r0 : r0 + 8, :]
        return solute_of(u, d, r, flux_sum(u, n, us, ns))

    strip_stage(strip_aniso, 2)
    strip_stage(strip_phase, 3)
    strip_stage(strip_solute, 4)
    for edge in edges:
        for t in range(TILES):
            v = edge[8 + 8 * t : 16 + 8 * t, :]
            edge[8 + 8 * t : 16 + 8 * t, :] = jnp.where(low, pltpu.roll(v, 127, 1), pltpu.roll(v, 1, 1))

    def near(buf, edge, q, r0, kept=None, keep=None):
        p = q & 15
        v = buf[p, pl.ds(r0, 8), :]
        if kept is None:
            e = pltpu.roll(edges[edge][pl.ds(r0, 8), :], 124 - 8 * p, 1)
            right = jnp.where(at127, e, pltpu.roll(v, 127, 1))
            left = jnp.where(at0, e, pltpu.roll(v, 1, 1))
        else:
            right = kept[0][p, pl.ds(r0, 8), :]
            left = kept[1][p, pl.ds(r0, 8), :]
        if keep is not None:
            keep[0][p, pl.ds(r0, 8), :] = right
            keep[1][p, pl.ds(r0, 8), :] = left
        return v, (
            buf[(q + 1) & 15, pl.ds(r0, 8), :],
            buf[(q - 1) & 15, pl.ds(r0, 8), :],
            buf[p, pl.ds(r0 + 1, 8), :],
            buf[p, pl.ds(r0 - 1, 8), :],
            right,
            left,
        )

    def stage(first, count, tiles, fn, unroll=2):
        def step(i, carry):
            for t in tiles:
                fn(shift + first + i, 8 + 8 * t)
            return carry

        lax.fori_loop(0, count, step, 0, unroll=unroll)

    def plane_aniso(q, r0):
        _, n = near(pb, 0, q, r0, keep=(pr_b, pl_b))
        ab[q & 15, pl.ds(r0, 8), :] = aniso_of(n[0] - n[1], n[2] - n[3], n[4] - n[5])

    def plane_phase(q, r0):
        p, ps = near(pb, 0, q, r0, kept=(pr_b, pl_b))
        a, as_ = near(ab, 2, q, r0)
        u = ub[q & 15, pl.ds(r0, 8), :]
        n, d, r = phase_of(p, a, u, flux_sum(p, a, ps, as_), thermal_of(DEPTH * gz + q))
        nb[q & 15, pl.ds(r0, 8), :] = n
        db[q & 15, pl.ds(r0, 8), :] = d
        rb[q & 15, pl.ds(r0, 8), :] = r

    def substep(buf, edge, q, r0, **held):
        u, us = near(buf, edge, q, r0)
        n, ns = near(nb, 3, q, r0, **held)
        return n, solute_of(u, db[q & 15, pl.ds(r0, 8), :], rb[q & 15, pl.ds(r0, 8), :], flux_sum(u, n, us, ns))

    def plane_first(q, r0):
        _, v = substep(ub, 1, q, r0, keep=(nr_b, nl_b))
        sb[q & 15, pl.ds(r0, 8), :] = v

    def plane_second(q, r0):
        n, v = substep(sb, 4, q, r0, kept=(nr_b, nl_b))
        outside = DEPTH * gz + q >= total
        phase_ref[q - shift, pl.ds(r0 - 16, 8), :] = jnp.where(outside, -1.0, 1.0 - n)
        solute_ref[q - shift, pl.ds(r0 - 16, 8), :] = jnp.where(outside, 0.0, v)

    every = range(TILES)
    stage(-3, 14, every, plane_aniso)
    stage(-2, 12, every, plane_phase)
    stage(-1, 10, every, plane_first)
    stage(0, 8, range(1, TILES - 1), plane_second)


def moved(value, axis, steps):
    count = lax.axis_size(axis)
    first, last = (max(0, -steps), min(count, count - steps))
    return lax.ppermute(value, axis, [(source, source + steps) for source in range(first, last)])


def out(*shape):
    return jax.ShapeDtypeStruct(shape, F32)


def call(kernel, shapes, n_smem, *args, scratch=()):
    return pl.pallas_call(
        kernel,
        out_shape=shapes,
        in_specs=[SMEM] * n_smem + [VMEM] * (len(args) - n_smem),
        out_specs=jax.tree.map(lambda _: VMEM, shapes),
        scratch_shapes=scratch,
        compiler_params=pltpu.CompilerParams(vmem_limit_bytes=40 * 1024 * 1024),
    )(*args)


def step_scratch():
    return [pltpu.VMEM((16, ROWS, 128), F32)] * 11 + [pltpu.VMEM((ROWS, 128), F32)] * 17


def branch(early, phase, solute, info):
    own_c, up8, down8 = call(pack_kernel, (out(128, 128), out(8, 8, 128), out(8, 8, 128)), 0, phase, solute)
    left = moved(own_c, "gx", 1)
    right = moved(own_c, "gx", -1)
    left, right, p, u = lax.optimization_barrier((left, right, phase, solute))
    near_p = moved(p[0:7] if early else p, "gz", -1)
    near_u = moved(u[0:5] if early else u, "gz", -1)
    if early:
        extra = moved(jnp.concatenate([p[5:8], u[7:8]]), "gz", 1)
    else:
        extra = moved(jnp.concatenate([p[0:4], u[0:2]]), "gz", -2)
    strip, up, down = call(
        strips_kernel, (out(128, 128), out(9, 8, 128), out(9, 8, 128)), 1, info, own_c, left, right, up8, down8
    )
    from_up = moved(up, "gy", 1)
    from_down = moved(down, "gy", -1)
    halo = call(halo_kernel, out(33, 8, 128), 1, info, from_up, from_down, up, down, strip)
    near_h = moved(halo, "gz", -1)
    extra_h = moved(halo, "gz", 1 if early else -2)
    return call(
        functools.partial(step_kernel, early),
        (out(*phase.shape), out(*phase.shape)),
        1,
        info,
        phase,
        solute,
        near_p,
        near_u,
        extra,
        halo,
        near_h,
        extra_h,
        scratch=step_scratch(),
    )


def body(phase, solute, advance):
    axes = ("gz", "gy", "gx")
    info = jnp.stack(
        [advance[0]] + [lax.axis_index(a) for a in axes] + [jnp.int32(lax.axis_size(a)) for a in axes]
    ).astype(jnp.int32)
    return lax.cond(
        advance[0] < 4, functools.partial(branch, True), functools.partial(branch, False), phase, solute, info
    )


def solution(mesh):
    in_specs = (P("gz", "gy", "gx"), P("gz", "gy", "gx"), P())
    out_specs = (P("gz", "gy", "gx"), P("gz", "gy", "gx"))
    return jax.shard_map(body, mesh=mesh, in_specs=in_specs, out_specs=out_specs, check_vma=False)
```

```python
import functools

import jax
import jax.numpy as jnp
from jax import lax
from jax.experimental import pallas as pl
from jax.experimental.pallas import tpu as pltpu
from jax.sharding import PartitionSpec as P

E_ANI = 0.05
FLOOR = 0.5
LAM = 1.6
DT = 0.1
DSOL = 0.5
KPART = 0.15
GTH = 2.0

F32 = jnp.float32
DEPTH = 8
ROWS = 160
TILES = 18
VMEM = pl.BlockSpec(memory_space=pltpu.VMEM)
SMEM = pl.BlockSpec(memory_space=pltpu.SMEM)


def lanes():
    return lax.broadcasted_iota(jnp.int32, (8, 128), 1)


def sublanes():
    return lax.broadcasted_iota(jnp.int32, (8, 128), 0)


def swapped(v, step, axis, index):
    size = v.shape[axis]
    return jnp.where((index & step) != 0, pltpu.roll(v, step, axis), pltpu.roll(v, size - step, axis))


def reversed_bits(v, steps, axis, index):
    for step in steps:
        if 2 * step == v.shape[axis]:
            v = pltpu.roll(v, step, axis)
        else:
            v = swapped(v, step, axis, index)
    return v


def reciprocal(v):
    r = pl.reciprocal(v, approx=True)
    return r * (2.0 - v * r)


def pack_kernel(p_ref, u_ref, c_ref):
    group = lanes() >> 3
    for t in range(16):
        acc = jnp.zeros((8, 128), F32)
        for f, ref in enumerate((p_ref, u_ref)):
            for z in range(DEPTH):
                v = pltpu.roll(ref[z, 8 * t : 8 * t + 8, :], 64 * f + 8 * z + 4, 1)
                acc = jnp.where(group == 8 * f + z, v, acc)
        c_ref[8 * t : 8 * t + 8, :] = acc


def rows_kernel(c_ref, p_ref, u_ref, up_ref, down_ref, m_ref):
    sub = sublanes()
    lane = lanes()
    for z in range(DEPTH):
        up_ref[z] = jnp.where(sub >= 4, p_ref[z, 120:128, :], pltpu.roll(u_ref[z, 120:128, :], 4, 0))
        down_ref[z] = jnp.where(sub < 4, p_ref[z, 0:8, :], pltpu.roll(u_ref[z, 0:8, :], 4, 0))
    for t in range(16):
        rows = slice(8 * t, 8 * t + 8)
        m_ref[rows, :] = reversed_bits(c_ref[rows, :], (1, 2, 4), 1, lane)


def strips_kernel(info_ref, m_ref, left_ref, right_ref, up8_ref, down8_ref, s_ref, up_ref, down_ref):
    lane = lanes()
    low = (lane & 4) == 0
    first = info_ref[3] == 0
    last = info_ref[3] == info_ref[6] - 1
    mirror = (low & first) | (jnp.logical_not(low) & last)
    for t in range(16):
        rows = slice(8 * t, 8 * t + 8)
        v = jnp.where(low, left_ref[rows, :], right_ref[rows, :])
        v = jnp.where(mirror, m_ref[rows, :], v)
        s_ref[rows, :] = v
        if t == 0:
            down_ref[8] = v
        if t == 15:
            up_ref[8] = v
    up_ref[0:8] = up8_ref[...]
    down_ref[0:8] = down8_ref[...]


def halo_kernel(info_ref, from_up_ref, from_down_ref, up_ref, down_ref, s_ref, h_ref):
    sub = sublanes()
    low = sub < 4
    first = info_ref[2] == 0
    last = info_ref[2] == info_ref[5] - 1
    for z in range(9):
        below = jnp.where(first, reversed_bits(down_ref[z], (1, 2, 4), 0, sub), from_up_ref[z])
        above = jnp.where(last, reversed_bits(up_ref[z], (1, 2, 4), 0, sub), from_down_ref[z])
        v = jnp.where(low, above, below)
        if z < 8:
            h_ref[z] = v
            h_ref[8 + z] = pltpu.roll(jnp.where(low, below, above), 4, 0)
        else:
            h_ref[32] = v
    for t in range(16):
        h_ref[16 + t] = s_ref[8 * t : 8 * t + 8, :]


CLASSES = ((1, 5, 3, 3, 1), (2, 7, 5, 2, 0), (4, 8, 6, 0, 0), (5, 8, 8, 2, 0), (7, 8, 8, 4, 2))
ORDER = [("p", z) for z in range(5)] + [("u", z) for z in range(3)]
ORDER += [("p", 5), ("u", 3), ("p", 6), ("u", 4), ("p", 7), ("u", 5), ("u", 6), ("u", 7)]


def step_kernel(
    kind,
    info_ref,
    p_ref,
    u_ref,
    next_ref,
    rest_ref,
    ex_ref,
    edge_ref,
    h_ref,
    hn_ref,
    phase_ref,
    solute_ref,
    pb,
    ub,
    ab,
    nb,
    db,
    rb,
    sb,
    pl_b,
    pr_b,
    nl_b,
    nr_b,
    *more,
):
    edges, strips = more[:5], more[5:]
    shift = info_ref[0]
    least, next_p, next_u, extra_p, extra_u = kind
    early = least < 4
    split = extra_p >= 3
    gz = info_ref[1]
    count_z = info_ref[4]
    total = DEPTH * count_z
    lane = lanes()
    group = lane >> 3
    low = (lane & 4) == 0
    at0 = lane == 0
    at127 = lane == 127
    is_first = gz == 0
    is_last = gz == count_z - 1
    is_second = gz == count_z - 2

    def place(buf, pos, plane, edge):
        buf[pos, 16:144, :] = plane
        buf[pos, 8:16, :] = edge
        buf[pos, 144:152, :] = edge

    def third(z):
        return edge_ref[z] if split else ex_ref[16 * (extra_p + extra_u) + z]

    for z in range(DEPTH):
        place(pb, z, p_ref[z], h_ref[z])
        place(ub, z, u_ref[z], h_ref[8 + z])
    for i in range(next_p + next_u):
        field, z = ORDER[i]
        src = rest_ref[i - 8] if split and i >= 8 else next_ref[i]
        place(pb if field == "p" else ub, 8 + z, src, hn_ref[z if field == "p" else 8 + z])

    for buf, extra, base, margin in ((pb, extra_p, 0, 4), (ub, extra_u, extra_p, 2)):
        for j in range(extra):
            pos = 16 - extra + j if early else j
            taken = pos >= 16 - margin + shift if early else pos <= shift + margin - 9

            @pl.when(taken)
            def _():
                for t in range(16):
                    buf[pos, 16 + 8 * t : 24 + 8 * t, :] = ex_ref[16 * (base + j) + t]
                edge = third(base + j)
                buf[pos, 8:16, :] = edge
                buf[pos, 144:152, :] = edge

            @pl.when(taken & (is_first if early else is_second))
            def _():
                buf[pos, 8:152, :] = buf[15 - pos, 8:152, :]

    @pl.when(is_last)
    def _():
        for pos in (8, 9, 10, 11):
            pb[pos, 8:152, :] = pb[15 - pos, 8:152, :]
            ub[pos, 8:152, :] = ub[15 - pos, 8:152, :]

    fresh = (group >= 12 + shift) if early else (group <= shift - 5)
    beyond = is_first if early else is_second
    mirror = (is_last & (group >= 8) & (group < 12)) | (fresh & beyond)
    for t in range(TILES):
        src = 16 if t in (0, TILES - 1) else t - 1
        rows = slice(8 + 8 * t, 16 + 8 * t)
        own, near = h_ref[16 + src], hn_ref[16 + src]
        cp = jnp.where(group < 8, own, pltpu.roll(near, 64, 1))
        cu = jnp.where(group < 8, pltpu.roll(own, 64, 1), near)
        if extra_p:
            far = third(extra_p + extra_u + src)
            far_r = pltpu.roll(far, 64, 1)
            cp = jnp.where(fresh, far_r if early else far, cp)
            cu = jnp.where(fresh, far if early else far_r, cu)
        edges[0][rows, :] = cp
        edges[1][rows, :] = cu

    @pl.when(is_last | beyond)
    def _():
        pick = group & 3
        for t in range(TILES):
            rows = slice(8 + 8 * t, 16 + 8 * t)
            for field in (0, 1):
                v = edges[field][rows, :]
                m = v
                for j in range(4):
                    amount = 8 * (2 * j + 1)
                    if early:
                        turned = pltpu.roll(v, jnp.where(is_first, 128 - amount, amount), 1)
                        m = jnp.where(pick == jnp.where(is_first, 3 - j, j), turned, m)
                    else:
                        m = jnp.where(pick == j, pltpu.roll(v, amount, 1), m)
                edges[field][rows, :] = jnp.where(mirror, m, v)

    for t in range(TILES):
        rows = slice(8 + 8 * t, 16 + 8 * t)
        cp = edges[0][rows, :]
        cu = edges[1][rows, :]
        gp = jnp.zeros((8, 128), F32)
        gu = jnp.zeros((8, 128), F32)
        for pos in range(16):
            gp = jnp.where(group == pos, pltpu.roll(pb[pos, rows, :], 8 * pos + 4, 1), gp)
        for pos in range(16):
            gu = jnp.where(group == pos, pltpu.roll(ub[pos, rows, :], 8 * pos + 4, 1), gu)
        strips[0][rows, :] = jnp.where(low, cp, gp)
        strips[1][rows, :] = jnp.where(low, gp, cp)
        strips[2][rows, :] = jnp.where(low, cu, gu)
        strips[3][rows, :] = jnp.where(low, gu, cu)

    def aniso_of(dz, dy, dx):
        sz, sy, sx = dz * dz, dy * dy, dx * dx
        floor = jnp.maximum(sz + sy + sx, 4.0 * FLOOR)
        ratio = (sz * sz + sy * sy + sx * sx) * reciprocal(floor * floor)
        factor = (1.0 - 3.0 * E_ANI) + (4.0 * E_ANI) * ratio
        return factor * factor

    def flux_sum(f, c, fs, cs):
        acc = None
        for near_f, near_c in zip(fs, cs):
            term = (c + near_c) * (near_f - f)
            acc = term if acc is None else acc + term
        return acc

    def phase_of(p, a, u, total_flux, thermal):
        om = 1.0 - p * p
        force = 0.5 * total_flux + om * (p - LAM * om * (u + thermal))
        new = jnp.clip(p + DT * (force * reciprocal(a)), -1.0, 1.0)
        den = 0.5 * (1.0 + KPART) - 0.5 * (1.0 - KPART) * new
        return 1.0 - new, new - p, 0.125 * DT * DSOL * reciprocal(den)

    def solute_of(u, d, r, total_flux):
        k = 0.5 / DT / (0.25 * DSOL)
        return u + r * (total_flux + (k + k * (1.0 - KPART) * u) * d)

    def thermal_of(g):
        g = jnp.where(g < 0, -1 - g, g)
        g = jnp.where(g >= total, 2 * total - 1 - g, g)
        return (GTH * (g.astype(F32) + 0.5 - total.astype(F32) / 2.0)) / total.astype(F32)

    q_lane = shift - 4 + ((group - (shift - 4)) & 15)
    strip_thermal = thermal_of(DEPTH * gz + q_lane)

    def strip_near(field, side, r0):
        v = strips[2 * field + side][r0 : r0 + 8, :]
        return v, (
            pltpu.roll(v, 120, 1),
            pltpu.roll(v, 8, 1),
            strips[2 * field + side][r0 + 1 : r0 + 9, :],
            strips[2 * field + side][r0 - 1 : r0 + 7, :],
            pltpu.roll(v, 127, 1),
            pltpu.roll(v, 1, 1),
        )

    def strip_stage(fn, edge):
        for t in range(TILES):
            r0 = 8 + 8 * t
            edges[edge][r0 : r0 + 8, :] = jnp.where(low, fn(0, r0), fn(1, r0))

    def strip_aniso(side, r0):
        _, n = strip_near(0, side, r0)
        a = aniso_of(n[0] - n[1], n[2] - n[3], n[4] - n[5])
        strips[4 + side][r0 : r0 + 8, :] = a
        return a

    def strip_phase(side, r0):
        p, ps = strip_near(0, side, r0)
        a, as_ = strip_near(2, side, r0)
        u = strips[2 + side][r0 : r0 + 8, :]
        n, d, r = phase_of(p, a, u, flux_sum(p, a, ps, as_), strip_thermal)
        strips[6 + side][r0 : r0 + 8, :] = n
        strips[8 + side][r0 : r0 + 8, :] = d
        strips[10 + side][r0 : r0 + 8, :] = r
        return n

    def strip_solute(side, r0):
        u, us = strip_near(1, side, r0)
        n, ns = strip_near(3, side, r0)
        d = strips[8 + side][r0 : r0 + 8, :]
        r = strips[10 + side][r0 : r0 + 8, :]
        return solute_of(u, d, r, flux_sum(u, n, us, ns))

    strip_stage(strip_aniso, 2)
    strip_stage(strip_phase, 3)
    strip_stage(strip_solute, 4)
    for edge in edges:
        for t in range(TILES):
            v = edge[8 + 8 * t : 16 + 8 * t, :]
            edge[8 + 8 * t : 16 + 8 * t, :] = jnp.where(low, pltpu.roll(v, 127, 1), pltpu.roll(v, 1, 1))

    def near(buf, edge, q, r0, kept=None, keep=None):
        p = q & 15
        v = buf[p, pl.ds(r0, 8), :]
        if kept is None:
            e = pltpu.roll(edges[edge][pl.ds(r0, 8), :], 124 - 8 * p, 1)
            right = jnp.where(at127, e, pltpu.roll(v, 127, 1))
            left = jnp.where(at0, e, pltpu.roll(v, 1, 1))
        else:
            right = kept[0][p, pl.ds(r0, 8), :]
            left = kept[1][p, pl.ds(r0, 8), :]
        if keep is not None:
            keep[0][p, pl.ds(r0, 8), :] = right
            keep[1][p, pl.ds(r0, 8), :] = left
        return v, (
            buf[(q + 1) & 15, pl.ds(r0, 8), :],
            buf[(q - 1) & 15, pl.ds(r0, 8), :],
            buf[p, pl.ds(r0 + 1, 8), :],
            buf[p, pl.ds(r0 - 1, 8), :],
            right,
            left,
        )

    def stage(first, count, tiles, fn, unroll=2):
        def step(i, carry):
            for t in tiles:
                fn(shift + first + i, 8 + 8 * t)
            return carry

        lax.fori_loop(0, count, step, 0, unroll=unroll)

    def plane_aniso(q, r0):
        _, n = near(pb, 0, q, r0, keep=(pr_b, pl_b))
        ab[q & 15, pl.ds(r0, 8), :] = aniso_of(n[0] - n[1], n[2] - n[3], n[4] - n[5])

    def plane_phase(q, r0):
        p, ps = near(pb, 0, q, r0, kept=(pr_b, pl_b))
        a, as_ = near(ab, 2, q, r0)
        u = ub[q & 15, pl.ds(r0, 8), :]
        n, d, r = phase_of(p, a, u, flux_sum(p, a, ps, as_), thermal_of(DEPTH * gz + q))
        nb[q & 15, pl.ds(r0, 8), :] = n
        db[q & 15, pl.ds(r0, 8), :] = d
        rb[q & 15, pl.ds(r0, 8), :] = r

    def substep(buf, edge, q, r0, **held):
        u, us = near(buf, edge, q, r0)
        n, ns = near(nb, 3, q, r0, **held)
        return n, solute_of(u, db[q & 15, pl.ds(r0, 8), :], rb[q & 15, pl.ds(r0, 8), :], flux_sum(u, n, us, ns))

    def plane_first(q, r0):
        _, v = substep(ub, 1, q, r0, keep=(nr_b, nl_b))
        sb[q & 15, pl.ds(r0, 8), :] = v

    def plane_second(q, r0):
        n, v = substep(sb, 4, q, r0, kept=(nr_b, nl_b))
        outside = DEPTH * gz + q >= total
        phase_ref[q - shift, pl.ds(r0 - 16, 8), :] = jnp.where(outside, -1.0, 1.0 - n)
        solute_ref[q - shift, pl.ds(r0 - 16, 8), :] = jnp.where(outside, 0.0, v)

    every = range(TILES)
    stage(-3, 14, every, plane_aniso)
    stage(-2, 12, every, plane_phase)
    stage(-1, 10, every, plane_first)
    stage(0, 8, range(1, TILES - 1), plane_second)


def moved(value, axis, steps):
    count = lax.axis_size(axis)
    first, last = (max(0, -steps), min(count, count - steps))
    return lax.ppermute(value, axis, [(source, source + steps) for source in range(first, last)])


def out(*shape):
    return jax.ShapeDtypeStruct(shape, F32)


def call(kernel, shapes, n_smem, *args, scratch=()):
    return pl.pallas_call(
        kernel,
        out_shape=shapes,
        in_specs=[SMEM] * n_smem + [VMEM] * (len(args) - n_smem),
        out_specs=jax.tree.map(lambda _: VMEM, shapes),
        scratch_shapes=scratch,
        compiler_params=pltpu.CompilerParams(vmem_limit_bytes=40 * 1024 * 1024),
    )(*args)


def step_scratch():
    return [pltpu.VMEM((16, ROWS, 128), F32)] * 11 + [pltpu.VMEM((ROWS, 128), F32)] * 17


def branch(kind, phase, solute, planes, info, left, right, mirrored, up8, down8):
    least, next_p, next_u, extra_p, extra_u = kind
    early = least < 4
    p = phase[DEPTH - extra_p :] if early else phase[:extra_p]
    u = solute[DEPTH - extra_u :] if early else solute[:extra_u]
    way = 1 if early else -2
    split = extra_p >= 3
    rest = planes[:1]
    if split:
        near = moved(planes[:8], "gz", -1)
        if next_p + next_u > 8:
            rest = moved(planes[8:], "gz", -1)
        main = moved(jnp.concatenate([p, u]).reshape(-1, 8, 128), "gz", way)
    else:
        near = moved(planes[: next_p + next_u], "gz", -1)
    strip, up, down = call(
        strips_kernel, (out(128, 128), out(9, 8, 128), out(9, 8, 128)), 1, info, mirrored, left, right, up8, down8
    )
    from_up = moved(up, "gy", 1)
    from_down = moved(down, "gy", -1)
    halo = call(halo_kernel, out(33, 8, 128), 1, info, from_up, from_down, up, down, strip)
    near_h = moved(halo, "gz", -1)
    far = halo
    edge = halo[:1]
    if extra_p:
        hp = halo[DEPTH - extra_p : DEPTH] if early else halo[:extra_p]
        hu = halo[2 * DEPTH - extra_u : 2 * DEPTH] if early else halo[DEPTH : DEPTH + extra_u]
        tiles = [hp, hu, halo[16:33]]
        if split:
            far, edge = main, moved(jnp.concatenate(tiles), "gz", way)
        else:
            far = moved(jnp.concatenate([v.reshape(-1, 8, 128) for v in (p, u)] + tiles), "gz", way)
    return call(
        functools.partial(step_kernel, kind),
        (out(*phase.shape), out(*phase.shape)),
        1,
        info,
        phase,
        solute,
        near,
        rest,
        far,
        edge,
        halo,
        near_h,
        scratch=step_scratch(),
    )


def body(phase, solute, advance):
    axes = ("gz", "gy", "gx")
    info = jnp.stack(
        [advance[0]] + [lax.axis_index(a) for a in axes] + [jnp.int32(lax.axis_size(a)) for a in axes]
    ).astype(jnp.int32)
    own_c = call(pack_kernel, out(128, 128), 0, phase, solute)
    left = moved(own_c, "gx", 1)
    right = moved(own_c, "gx", -1)
    up8, down8, mirrored = call(
        rows_kernel, (out(8, 8, 128), out(8, 8, 128), out(128, 128)), 0, own_c, phase, solute
    )
    planes = jnp.stack([(phase if field == "p" else solute)[z] for field, z in ORDER])
    index = sum((advance[0] >= kind[0]).astype(jnp.int32) for kind in CLASSES[1:])
    branches = [functools.partial(branch, kind) for kind in CLASSES]
    return lax.switch(index, branches, phase, solute, planes, info, left, right, mirrored, up8, down8)


def solution(mesh):
    in_specs = (P("gz", "gy", "gx"), P("gz", "gy", "gx"), P())
    out_specs = (P("gz", "gy", "gx"), P("gz", "gy", "gx"))
    return jax.shard_map(body, mesh=mesh, in_specs=in_specs, out_specs=out_specs, check_vma=False)
```

```python
import functools

import jax
import jax.numpy as jnp
from jax import lax
from jax.experimental import pallas as pl
from jax.experimental.pallas import tpu as pltpu
from jax.sharding import PartitionSpec as P

E_ANI = 0.05
FLOOR = 0.5
LAM = 1.6
DT = 0.1
DSOL = 0.5
KPART = 0.15
GTH = 2.0

F32 = jnp.float32
DEPTH = 8
ROWS = 160
TILES = 18
VMEM = pl.BlockSpec(memory_space=pltpu.VMEM)
SMEM = pl.BlockSpec(memory_space=pltpu.SMEM)


def lanes():
    return lax.broadcasted_iota(jnp.int32, (8, 128), 1)


def sublanes():
    return lax.broadcasted_iota(jnp.int32, (8, 128), 0)


def swapped(v, step, axis, index):
    size = v.shape[axis]
    return jnp.where((index & step) != 0, pltpu.roll(v, step, axis), pltpu.roll(v, size - step, axis))


def reversed_bits(v, steps, axis, index):
    for step in steps:
        if 2 * step == v.shape[axis]:
            v = pltpu.roll(v, step, axis)
        else:
            v = swapped(v, step, axis, index)
    return v


def reciprocal(v):
    r = pl.reciprocal(v, approx=True)
    return r * (2.0 - v * r)


def pack_kernel(p_ref, u_ref, c_ref):
    group = lanes() >> 3
    for t in range(16):
        acc = jnp.zeros((8, 128), F32)
        for f, ref in enumerate((p_ref, u_ref)):
            for z in range(DEPTH):
                v = pltpu.roll(ref[z, 8 * t : 8 * t + 8, :], 64 * f + 8 * z + 4, 1)
                acc = jnp.where(group == 8 * f + z, v, acc)
        c_ref[8 * t : 8 * t + 8, :] = acc


def rows_kernel(c_ref, p_ref, u_ref, up_ref, down_ref, m_ref):
    sub = sublanes()
    lane = lanes()
    for z in range(DEPTH):
        up_ref[z] = jnp.where(sub >= 4, p_ref[z, 120:128, :], pltpu.roll(u_ref[z, 120:128, :], 4, 0))
        down_ref[z] = jnp.where(sub < 4, p_ref[z, 0:8, :], pltpu.roll(u_ref[z, 0:8, :], 4, 0))
    for t in range(16):
        rows = slice(8 * t, 8 * t + 8)
        m_ref[rows, :] = reversed_bits(c_ref[rows, :], (1, 2, 4), 1, lane)


def strips_kernel(info_ref, m_ref, left_ref, right_ref, up8_ref, down8_ref, s_ref, up_ref, down_ref):
    lane = lanes()
    low = (lane & 4) == 0
    first = info_ref[3] == 0
    last = info_ref[3] == info_ref[6] - 1
    mirror = (low & first) | (jnp.logical_not(low) & last)
    for t in range(16):
        rows = slice(8 * t, 8 * t + 8)
        v = jnp.where(low, left_ref[rows, :], right_ref[rows, :])
        v = jnp.where(mirror, m_ref[rows, :], v)
        s_ref[rows, :] = v
        if t == 0:
            down_ref[8] = v
        if t == 15:
            up_ref[8] = v
    up_ref[0:8] = up8_ref[...]
    down_ref[0:8] = down8_ref[...]


def halo_kernel(info_ref, from_up_ref, from_down_ref, up_ref, down_ref, s_ref, h_ref):
    sub = sublanes()
    low = sub < 4
    first = info_ref[2] == 0
    last = info_ref[2] == info_ref[5] - 1
    for z in range(9):
        below = jnp.where(first, reversed_bits(down_ref[z], (1, 2, 4), 0, sub), from_up_ref[z])
        above = jnp.where(last, reversed_bits(up_ref[z], (1, 2, 4), 0, sub), from_down_ref[z])
        v = jnp.where(low, above, below)
        if z < 8:
            h_ref[z] = v
            h_ref[8 + z] = pltpu.roll(jnp.where(low, below, above), 4, 0)
        else:
            h_ref[32] = v
    for t in range(16):
        h_ref[16 + t] = s_ref[8 * t : 8 * t + 8, :]


CLASSES = ((1, 5, 3, 3, 1), (2, 7, 5, 2, 0), (4, 8, 6, 0, 0), (5, 8, 8, 2, 0), (7, 8, 8, 4, 2))
ORDER = [("p", z) for z in range(5)] + [("u", z) for z in range(3)]
ORDER += [("p", 5), ("u", 3), ("p", 6), ("u", 4), ("p", 7), ("u", 5), ("u", 6), ("u", 7)]


def step_kernel(
    kind,
    info_ref,
    p_ref,
    u_ref,
    next_ref,
    rest_ref,
    ex_ref,
    edge_ref,
    h_ref,
    hn_ref,
    phase_ref,
    solute_ref,
    pb,
    ub,
    ab,
    nb,
    db,
    rb,
    sb,
    pl_b,
    pr_b,
    nl_b,
    nr_b,
    *more,
):
    edges, strips = more[:5], more[5:]
    shift = info_ref[0]
    least, next_p, next_u, extra_p, extra_u = kind
    early = least < 4
    split = extra_p >= 3
    gz = info_ref[1]
    count_z = info_ref[4]
    total = DEPTH * count_z
    lane = lanes()
    group = lane >> 3
    low = (lane & 4) == 0
    at0 = lane == 0
    at127 = lane == 127
    is_first = gz == 0
    is_last = gz == count_z - 1
    is_second = gz == count_z - 2

    def place(buf, pos, plane, edge):
        buf[pos, 16:144, :] = plane
        buf[pos, 8:16, :] = edge
        buf[pos, 144:152, :] = edge

    def third(z):
        return edge_ref[z] if split else ex_ref[16 * (extra_p + extra_u) + z]

    for z in range(DEPTH):
        place(pb, z, p_ref[z], h_ref[z])
        place(ub, z, u_ref[z], h_ref[8 + z])
    for i in range(next_p + next_u):
        field, z = ORDER[i]
        src = rest_ref[i - 8] if split and i >= 8 else next_ref[i]
        place(pb if field == "p" else ub, 8 + z, src, hn_ref[z if field == "p" else 8 + z])

    for buf, extra, base, margin in ((pb, extra_p, 0, 4), (ub, extra_u, extra_p, 2)):
        for j in range(extra):
            pos = 16 - extra + j if early else j
            taken = pos >= 16 - margin + shift if early else pos <= shift + margin - 9

            @pl.when(taken)
            def _():
                for t in range(16):
                    buf[pos, 16 + 8 * t : 24 + 8 * t, :] = ex_ref[16 * (base + j) + t]
                edge = third(base + j)
                buf[pos, 8:16, :] = edge
                buf[pos, 144:152, :] = edge

            @pl.when(taken & (is_first if early else is_second))
            def _():
                buf[pos, 8:152, :] = buf[15 - pos, 8:152, :]

    @pl.when(is_last)
    def _():
        for pos in (8, 9, 10, 11):
            pb[pos, 8:152, :] = pb[15 - pos, 8:152, :]
            ub[pos, 8:152, :] = ub[15 - pos, 8:152, :]

    fresh = (group >= 12 + shift) if early else (group <= shift - 5)
    beyond = is_first if early else is_second
    mirror = (is_last & (group >= 8) & (group < 12)) | (fresh & beyond)
    for t in range(TILES):
        src = 16 if t in (0, TILES - 1) else t - 1
        rows = slice(8 + 8 * t, 16 + 8 * t)
        own, near = h_ref[16 + src], hn_ref[16 + src]
        cp = jnp.where(group < 8, own, pltpu.roll(near, 64, 1))
        cu = jnp.where(group < 8, pltpu.roll(own, 64, 1), near)
        if extra_p:
            far = third(extra_p + extra_u + src)
            far_r = pltpu.roll(far, 64, 1)
            cp = jnp.where(fresh, far_r if early else far, cp)
            cu = jnp.where(fresh, far if early else far_r, cu)
        edges[0][rows, :] = cp
        edges[1][rows, :] = cu

    @pl.when(is_last | beyond)
    def _():
        pick = group & 3
        for t in range(TILES):
            rows = slice(8 + 8 * t, 16 + 8 * t)
            for field in (0, 1):
                v = edges[field][rows, :]
                m = v
                for j in range(4):
                    amount = 8 * (2 * j + 1)
                    if early:
                        turned = pltpu.roll(v, jnp.where(is_first, 128 - amount, amount), 1)
                        m = jnp.where(pick == jnp.where(is_first, 3 - j, j), turned, m)
                    else:
                        m = jnp.where(pick == j, pltpu.roll(v, amount, 1), m)
                edges[field][rows, :] = jnp.where(mirror, m, v)

    for t in range(TILES):
        rows = slice(8 + 8 * t, 16 + 8 * t)
        cp = edges[0][rows, :]
        cu = edges[1][rows, :]
        gp = jnp.zeros((8, 128), F32)
        gu = jnp.zeros((8, 128), F32)
        for pos in range(16):
            gp = jnp.where(group == pos, pltpu.roll(pb[pos, rows, :], 8 * pos + 4, 1), gp)
        for pos in range(16):
            gu = jnp.where(group == pos, pltpu.roll(ub[pos, rows, :], 8 * pos + 4, 1), gu)
        strips[0][rows, :] = jnp.where(low, cp, gp)
        strips[1][rows, :] = jnp.where(low, gp, cp)
        strips[2][rows, :] = jnp.where(low, cu, gu)
        strips[3][rows, :] = jnp.where(low, gu, cu)

    def aniso_of(dz, dy, dx):
        sz, sy, sx = dz * dz, dy * dy, dx * dx
        floor = jnp.maximum(sz + sy + sx, 4.0 * FLOOR)
        ratio = (sz * sz + sy * sy + sx * sx) * reciprocal(floor * floor)
        factor = (1.0 - 3.0 * E_ANI) + (4.0 * E_ANI) * ratio
        return factor * factor

    def flux_sum(f, c, fs, cs):
        acc = None
        for near_f, near_c in zip(fs, cs):
            term = (c + near_c) * (near_f - f)
            acc = term if acc is None else acc + term
        return acc

    def phase_of(p, a, u, total_flux, thermal):
        om = 1.0 - p * p
        force = 0.5 * total_flux + om * (p - LAM * om * (u + thermal))
        new = jnp.clip(p + DT * (force * reciprocal(a)), -1.0, 1.0)
        den = 0.5 * (1.0 + KPART) - 0.5 * (1.0 - KPART) * new
        return 1.0 - new, new - p, 0.125 * DT * DSOL * reciprocal(den)

    def solute_of(u, d, r, total_flux):
        k = 0.5 / DT / (0.25 * DSOL)
        return u + r * (total_flux + (k + k * (1.0 - KPART) * u) * d)

    def thermal_of(g):
        g = jnp.where(g < 0, -1 - g, g)
        g = jnp.where(g >= total, 2 * total - 1 - g, g)
        return (GTH * (g.astype(F32) + 0.5 - total.astype(F32) / 2.0)) / total.astype(F32)

    q_lane = shift - 4 + ((group - (shift - 4)) & 15)
    strip_thermal = thermal_of(DEPTH * gz + q_lane)

    def strip_near(field, side, r0):
        v = strips[2 * field + side][r0 : r0 + 8, :]
        return v, (
            pltpu.roll(v, 120, 1),
            pltpu.roll(v, 8, 1),
            strips[2 * field + side][r0 + 1 : r0 + 9, :],
            strips[2 * field + side][r0 - 1 : r0 + 7, :],
            pltpu.roll(v, 127, 1),
            pltpu.roll(v, 1, 1),
        )

    def strip_stage(fn, edge):
        for t in range(TILES):
            r0 = 8 + 8 * t
            edges[edge][r0 : r0 + 8, :] = jnp.where(low, fn(0, r0), fn(1, r0))

    def strip_aniso(side, r0):
        _, n = strip_near(0, side, r0)
        a = aniso_of(n[0] - n[1], n[2] - n[3], n[4] - n[5])
        strips[4 + side][r0 : r0 + 8, :] = a
        return a

    def strip_phase(side, r0):
        p, ps = strip_near(0, side, r0)
        a, as_ = strip_near(2, side, r0)
        u = strips[2 + side][r0 : r0 + 8, :]
        n, d, r = phase_of(p, a, u, flux_sum(p, a, ps, as_), strip_thermal)
        strips[6 + side][r0 : r0 + 8, :] = n
        strips[8 + side][r0 : r0 + 8, :] = d
        strips[10 + side][r0 : r0 + 8, :] = r
        return n

    def strip_solute(side, r0):
        u, us = strip_near(1, side, r0)
        n, ns = strip_near(3, side, r0)
        d = strips[8 + side][r0 : r0 + 8, :]
        r = strips[10 + side][r0 : r0 + 8, :]
        return solute_of(u, d, r, flux_sum(u, n, us, ns))

    strip_stage(strip_aniso, 2)
    strip_stage(strip_phase, 3)
    strip_stage(strip_solute, 4)
    for edge in edges:
        for t in range(TILES):
            v = edge[8 + 8 * t : 16 + 8 * t, :]
            edge[8 + 8 * t : 16 + 8 * t, :] = jnp.where(low, pltpu.roll(v, 127, 1), pltpu.roll(v, 1, 1))

    def near(buf, edge, q, r0, kept=None, keep=None):
        p = q & 15
        v = buf[p, pl.ds(r0, 8), :]
        if kept is None:
            e = pltpu.roll(edges[edge][pl.ds(r0, 8), :], 124 - 8 * p, 1)
            right = jnp.where(at127, e, pltpu.roll(v, 127, 1))
            left = jnp.where(at0, e, pltpu.roll(v, 1, 1))
        else:
            right = kept[0][p, pl.ds(r0, 8), :]
            left = kept[1][p, pl.ds(r0, 8), :]
        if keep is not None:
            keep[0][p, pl.ds(r0, 8), :] = right
            keep[1][p, pl.ds(r0, 8), :] = left
        return v, (
            buf[(q + 1) & 15, pl.ds(r0, 8), :],
            buf[(q - 1) & 15, pl.ds(r0, 8), :],
            buf[p, pl.ds(r0 + 1, 8), :],
            buf[p, pl.ds(r0 - 1, 8), :],
            right,
            left,
        )

    def stage(first, count, tiles, fn, unroll=2):
        def step(i, carry):
            for t in tiles:
                fn(shift + first + i, 8 + 8 * t)
            return carry

        lax.fori_loop(0, count, step, 0, unroll=unroll)

    def plane_aniso(q, r0):
        _, n = near(pb, 0, q, r0, keep=(pr_b, pl_b))
        ab[q & 15, pl.ds(r0, 8), :] = aniso_of(n[0] - n[1], n[2] - n[3], n[4] - n[5])

    def plane_phase(q, r0):
        p, ps = near(pb, 0, q, r0, kept=(pr_b, pl_b))
        a, as_ = near(ab, 2, q, r0)
        u = ub[q & 15, pl.ds(r0, 8), :]
        n, d, r = phase_of(p, a, u, flux_sum(p, a, ps, as_), thermal_of(DEPTH * gz + q))
        nb[q & 15, pl.ds(r0, 8), :] = n
        db[q & 15, pl.ds(r0, 8), :] = d
        rb[q & 15, pl.ds(r0, 8), :] = r

    def substep(buf, edge, q, r0, **held):
        u, us = near(buf, edge, q, r0)
        n, ns = near(nb, 3, q, r0, **held)
        return n, solute_of(u, db[q & 15, pl.ds(r0, 8), :], rb[q & 15, pl.ds(r0, 8), :], flux_sum(u, n, us, ns))

    def plane_first(q, r0):
        _, v = substep(ub, 1, q, r0, keep=(nr_b, nl_b))
        sb[q & 15, pl.ds(r0, 8), :] = v

    def plane_second(q, r0):
        n, v = substep(sb, 4, q, r0, kept=(nr_b, nl_b))
        outside = DEPTH * gz + q >= total
        phase_ref[q - shift, pl.ds(r0 - 16, 8), :] = jnp.where(outside, -1.0, 1.0 - n)
        solute_ref[q - shift, pl.ds(r0 - 16, 8), :] = jnp.where(outside, 0.0, v)

    every = range(TILES)
    stage(-3, 14, every, plane_aniso)
    stage(-2, 12, every, plane_phase)
    stage(-1, 10, every, plane_first)
    stage(0, 8, range(1, TILES - 1), plane_second)


def moved(value, axis, steps):
    count = lax.axis_size(axis)
    first, last = (max(0, -steps), min(count, count - steps))
    return lax.ppermute(value, axis, [(source, source + steps) for source in range(first, last)])


def out(*shape):
    return jax.ShapeDtypeStruct(shape, F32)


def call(kernel, shapes, n_smem, *args, scratch=()):
    return pl.pallas_call(
        kernel,
        out_shape=shapes,
        in_specs=[SMEM] * n_smem + [VMEM] * (len(args) - n_smem),
        out_specs=jax.tree.map(lambda _: VMEM, shapes),
        scratch_shapes=scratch,
        compiler_params=pltpu.CompilerParams(vmem_limit_bytes=40 * 1024 * 1024),
    )(*args)


def step_scratch():
    return [pltpu.VMEM((16, ROWS, 128), F32)] * 11 + [pltpu.VMEM((ROWS, 128), F32)] * 17


def first_hop(planes):
    return lax.ppermute(planes, "gz", [(i, i - 2) for i in range(2, lax.axis_size("gz"), 2)])


def second_hop(planes, held, place):
    count = lax.axis_size("gz")
    odd = lax.rem(place, 2) == 1
    pairs = [(i, i - 1) for i in range(1, count, 2)] + [(i, i + 1) for i in range(0, count - 1, 2)]
    return lax.ppermute(jnp.where(odd, planes, held), "gz", pairs)


def branch(kind, phase, solute, planes, info, left, right, mirrored, up8, down8):
    least, next_p, next_u, extra_p, extra_u = kind
    early = least < 4
    p = phase[DEPTH - extra_p :] if early else phase[:extra_p]
    u = solute[DEPTH - extra_u :] if early else solute[:extra_u]
    way = 1 if early else -2
    split = extra_p >= 3
    rest = planes[:1]
    if split:
        near = moved(planes[:8], "gz", -1)
        if next_p + next_u > 8:
            held = first_hop(planes[8:])
        main = moved(jnp.concatenate([p, u]).reshape(-1, 8, 128), "gz", way)
    else:
        near = moved(planes[: next_p + next_u], "gz", -1)
    strip, up, down = call(
        strips_kernel, (out(128, 128), out(9, 8, 128), out(9, 8, 128)), 1, info, mirrored, left, right, up8, down8
    )
    from_up = moved(up, "gy", 1)
    from_down = moved(down, "gy", -1)
    halo = call(halo_kernel, out(33, 8, 128), 1, info, from_up, from_down, up, down, strip)
    near_h = moved(halo, "gz", -1)
    if split and next_p + next_u > 8:
        held, near, _ = lax.optimization_barrier((held, near, halo))
        rest = second_hop(planes[8:], held, info[1])
    far = halo
    edge = halo[:1]
    if extra_p:
        hp = halo[DEPTH - extra_p : DEPTH] if early else halo[:extra_p]
        hu = halo[2 * DEPTH - extra_u : 2 * DEPTH] if early else halo[DEPTH : DEPTH + extra_u]
        tiles = [hp, hu, halo[16:33]]
        if split:
            far, edge = main, moved(jnp.concatenate(tiles), "gz", way)
        else:
            far = moved(jnp.concatenate([v.reshape(-1, 8, 128) for v in (p, u)] + tiles), "gz", way)
    return call(
        functools.partial(step_kernel, kind),
        (out(*phase.shape), out(*phase.shape)),
        1,
        info,
        phase,
        solute,
        near,
        rest,
        far,
        edge,
        halo,
        near_h,
        scratch=step_scratch(),
    )


def body(phase, solute, advance):
    axes = ("gz", "gy", "gx")
    info = jnp.stack(
        [advance[0]] + [lax.axis_index(a) for a in axes] + [jnp.int32(lax.axis_size(a)) for a in axes]
    ).astype(jnp.int32)
    own_c = call(pack_kernel, out(128, 128), 0, phase, solute)
    left = moved(own_c, "gx", 1)
    right = moved(own_c, "gx", -1)
    up8, down8, mirrored = call(
        rows_kernel, (out(8, 8, 128), out(8, 8, 128), out(128, 128)), 0, own_c, phase, solute
    )
    planes = jnp.stack([(phase if field == "p" else solute)[z] for field, z in ORDER])
    index = sum((advance[0] >= kind[0]).astype(jnp.int32) for kind in CLASSES[1:])
    branches = [functools.partial(branch, kind) for kind in CLASSES]
    return lax.switch(index, branches, phase, solute, planes, info, left, right, mirrored, up8, down8)


def solution(mesh):
    in_specs = (P("gz", "gy", "gx"), P("gz", "gy", "gx"), P())
    out_specs = (P("gz", "gy", "gx"), P("gz", "gy", "gx"))
    return jax.shard_map(body, mesh=mesh, in_specs=in_specs, out_specs=out_specs, check_vma=False)
```
